128 devices in a mesh: dp: 8 (over y_lo, z), tp: 16 (over x, y_hi, core).
Axes of the slice: x: 4, y: 4 (y_hi: 2, y_lo: 2; y = y_hi * 2 + y_lo), z: 4, core: 2. Of those that a mesh axis runs over, the one named last changes fastest.
Arguments:
- queries: bfloat16 [4096, 128, 576], P(('dp', 'tp')), may hold values from -16 to 16
- new_latent: bfloat16 [4096, 576], P(('dp', 'tp')), may hold values from -6 to 6
- latent_cache: bfloat16 [4096, 384, 576], P(('dp', 'tp')), may hold values from -6 to 6
- lengths: int32 [4096], P(('dp', 'tp')), may hold values from 1 to 384, 524288 in all
- residual: bfloat16 [4096, 7168], P(('dp', 'tp')), may hold values from -1.1953125 to 1.1953125
- value_up: bfloat16 [128, 512, 128], P('tp'), may hold values from -0.25 to 0.25
- out_proj: bfloat16 [16384, 7168], P('tp'), may hold values from -0.046875 to 0.046875
- norm_gain: bfloat16 [7168], replicated, may hold values from 0.5 to 1.5
Outputs:
- hidden: bfloat16 [4096, 7168], P(('dp', 'tp'))
- normed: bfloat16 [4096, 7168], P(('dp', 'tp'))
The draws below stay inside these ranges and needn't reach their ends.
Inputs may be any that keep to these rules, and one draw needn't show every extreme that they name: `lengths`: slots at or past a request's length hold stale entries that are not read.
All inputs are finite; a program needn't handle non-finite values. No bound on the sum of `lengths` on one device may be relied on, other than what follows from the above.
Results may differ from the reference program's by a relative error of at most 0.02.
Values may be sent and summed in bfloat16 or wider, within the bound.
No kernel may reach another device: no remote copies, remote signals or barrier semaphores. Data moves between devices by JAX's collectives and lax.ppermute only.
A program may use at most 192 MiB of HBM per device.

```python
import math
import jax
import jax.numpy as jnp
import numpy as np
from jax import lax

D = 7168
H = 128
KVL = 512
ROPE = 64
HD = 128
REQ_DEV = 32
MAXLEN = 384
REQUESTS = 4096
N_TP = 16


def shared_uniform(key):
    return jax.random.uniform(key, (REQUESTS, KVL + ROPE), jnp.float32, 1e-06, 1.0 - 1e-06)


def draw_new_latent(key, part):
    base = shared_uniform(key)
    key = jax.random.fold_in(key, 5)
    angles = jax.random.uniform(key, (REQUESTS, KVL + ROPE), jnp.float32, 0.0, 1.0)
    return (jnp.sqrt(-2.0 * jnp.log(base)) * jnp.cos(2.0 * math.pi * angles)).astype(jnp.bfloat16)


def draw_queries(key, part):
    key = jax.random.fold_in(key, 11)
    noise_key = jax.random.fold_in(key, 0)
    return (0.5 * jax.random.normal(noise_key, (REQUESTS, H, KVL + ROPE), jnp.float32)).astype(jnp.bfloat16)


def draw_latent_cache(key, part):
    key = jax.random.fold_in(key, 23)
    return jnp.clip(jax.random.normal(key, (REQUESTS, MAXLEN, KVL + ROPE), jnp.float32), -6.0, 6.0).astype(jnp.bfloat16)


def levels(key, dims, pieces, low, top_value):
    def one(axis_at, parts):
        steps = jax.random.uniform(jax.random.fold_in(jax.random.fold_in(key, 6), axis_at), (parts,), jnp.float32, low / len(pieces), top_value / len(pieces))
        return jnp.repeat(jnp.exp(steps), dims[axis_at] // parts).reshape((-1,) + (1,) * (len(dims) - axis_at - 1))

    factor_of = one(*pieces[0])
    for cut in pieces[1:]:
        factor_of = factor_of * one(*cut)
    return factor_of


def split_up(count, total, limit, skew):
    portions = [(1 << 20) // math.isqrt(standing ** skew) + 1 for standing in range(2, count + 1)]
    surplus, holding = total - limit - (count - 1), [1] * (count - 1)
    while surplus > 0:
        movable = [i for i in range(count - 1) if holding[i] < limit]
        pool, left = sum([portions[i] for i in movable]), surplus
        for i in movable:
            extra = min(limit - holding[i], max(1, left * portions[i] // pool), surplus)
            holding[i] = holding[i] + extra
            surplus = surplus - extra
    return np.array([limit] + holding)


def uneven(rng, count, total, most, skew):
    if count == 2:
        one = jax.random.randint(rng, (), max(1, total - most), min(most, total - 1) + 1)
        return jnp.stack([one, total - one])
    sizes = jnp.asarray(split_up(count, total, most, skew), jnp.int32)
    couples = (count - 1) // 2
    donor, receiver = sizes[1:1 + 2 * couples:2], sizes[2:2 + 2 * couples:2]
    room = jnp.minimum(donor - 1, most - receiver)
    moved = jax.random.randint(jax.random.fold_in(rng, 1), (couples,), 0, 1 << 20) % (room + 1)
    sizes = sizes.at[1:1 + 2 * couples:2].set(donor - moved).at[2:2 + 2 * couples:2].set(receiver + moved)
    return sizes[jax.random.permutation(jax.random.fold_in(rng, 2), count)]


def noise(key, dims, scale, most, shards=(), kind=jnp.bfloat16):
    result = jax.random.normal(key, dims, jnp.float32) * scale
    if len(shards) > 0:
        result = levels(key, dims, shards, -0.22, 0.18) * result
    return jnp.clip(result, min=-most, max=most).astype(kind)


def setup_inputs(seed: int = 0) -> dict:
    arg_keys = jax.random.split(jax.random.key(seed), 9)
    return {
        "queries": draw_queries(jax.random.fold_in(arg_keys[8], 71), 0),
        "new_latent": draw_new_latent(jax.random.fold_in(arg_keys[8], 71), 0),
        "latent_cache": draw_latent_cache(jax.random.fold_in(arg_keys[8], 71), 0),
        "lengths": uneven(arg_keys[3], REQUESTS, REQUESTS * MAXLEN // 3, MAXLEN, 2).astype(jnp.int32),
        "residual": noise(arg_keys[4], (REQUESTS, D), 0.2, 1.1953125, ((0, 128),)),
        "value_up": noise(arg_keys[5], (H, KVL, HD), KVL ** -0.5, 0.25, ((0, 16),)),
        "out_proj": noise(arg_keys[6], (H * HD, D), (H * HD) ** -0.5, 0.046875, ((0, 16),)),
        "norm_gain": jnp.clip(1.0 + 0.1 * jax.random.normal(arg_keys[7], (D,), jnp.float32), 0.5, 1.5).astype(jnp.bfloat16),
    }


softmax_scale = 0.1353
epsilon = 1e-06

def attend_block(inputs):
    queries, new_latent, latent_cache, lengths = inputs
    query_wide = queries.astype(jnp.float32)
    cache_wide = latent_cache.astype(jnp.float32)
    new_wide = new_latent.astype(jnp.float32)
    scores = jnp.einsum('bhc,blc->bhl', query_wide, cache_wide) * softmax_scale
    new_score = jnp.einsum('bhc,bc->bh', query_wide, new_wide) * softmax_scale
    positions = jnp.arange(latent_cache.shape[1], dtype=jnp.int32)
    visible = positions[None, None, :] < lengths[:, None, None]
    masked = jnp.where(visible, scores, -1e+30)
    maxima = jnp.maximum(lax.optimization_barrier(jnp.max(masked, axis=2)), new_score)
    probs = jnp.where(visible, jnp.exp(masked - maxima[:, :, None]), 0.0)
    new_prob = jnp.exp(new_score - maxima)
    totals = lax.optimization_barrier(jnp.sum(probs, axis=2)) + new_prob
    probs_low = lax.optimization_barrier(probs.astype(jnp.bfloat16)).astype(jnp.float32)
    new_low = lax.optimization_barrier(new_prob.astype(jnp.bfloat16)).astype(jnp.float32)
    summed = jnp.einsum('bhl,bld->bhd', probs_low, cache_wide[:, :, :KVL])
    summed = summed + new_low[:, :, None] * new_wide[:, None, :KVL]
    return (summed / totals[:, :, None]).astype(jnp.bfloat16)

def reference(queries, new_latent, latent_cache, lengths, residual, value_up, out_proj, norm_gain):
    group_rows = REQ_DEV * N_TP
    block_count = REQUESTS // group_rows
    stacked = (queries.reshape(block_count, group_rows, H, KVL + ROPE), new_latent.reshape(block_count, group_rows, KVL + ROPE), latent_cache.reshape(block_count, group_rows, MAXLEN, KVL + ROPE), lengths.reshape(block_count, group_rows))
    attended = lax.map(attend_block, stacked).reshape(REQUESTS, H, KVL)
    head_values = jnp.einsum('bhk,hkd->bhd', attended.astype(jnp.float32), value_up.astype(jnp.float32)).astype(jnp.bfloat16)
    projected = jnp.dot(head_values.reshape(REQUESTS, H * HD), out_proj, preferred_element_type=jnp.float32)
    hidden = (residual.astype(jnp.float32) + projected).astype(jnp.bfloat16)
    widened = lax.optimization_barrier(hidden).astype(jnp.float32)
    mean_square = lax.optimization_barrier(jnp.mean(widened * widened, axis=1, keepdims=True))
    normed = (widened * lax.rsqrt(mean_square + epsilon) * norm_gain.astype(jnp.float32)).astype(jnp.bfloat16)
    return (hidden, normed)
```

```python
import functools

import jax
import jax.numpy as jnp
from jax import lax
from jax.experimental import pallas as pl
from jax.experimental.pallas import tpu as pltpu
from jax.sharding import PartitionSpec as P

softmax_scale = 0.1353
masked_score = -1e30
epsilon = 1e-06

N_X, N_Y, N_CORE = 4, 2, 2
STEP = 4
TILE = 512
WHOLE = pl.BlockSpec(memory_space=pltpu.VMEM)


def moved(array, dx=0, dy=0, dcore=0):
    pairs = []
    for t in range(N_X * N_Y * N_CORE):
        x, y, core = t // (N_Y * N_CORE), t // N_CORE % N_Y, t % N_CORE
        to = ((x + dx) % N_X * N_Y + (y ^ dy)) * N_CORE + (core ^ dcore)
        pairs.append((t, to))
    return lax.ppermute(array, "tp", pairs)


def attend_kernel(first, rows, latent, len_ref, group_ref, q_ref, c_ref, n_ref, *rest):
    outs, (stage, new_wide) = rest[:-2], rest[-2:]
    i = pl.program_id(0)
    heads, slots = q_ref.shape[2], c_ref.shape[2]

    @pl.when(i == 0)
    def _():
        new_wide[...] = n_ref[...].astype(jnp.float32)

    def attend_to(seen):
        every = range(STEP)
        queries = [q_ref[j].T for j in every]
        keys = [c_ref[j, :, :seen] for j in every]
        news = [new_wide[pl.ds(first + i * STEP + j, 1), :] for j in every]
        scores = [
            jnp.dot(q, k, preferred_element_type=jnp.float32) * softmax_scale
            for q, k in zip(queries, keys)
        ]
        new_scores = [
            jnp.sum(q.astype(jnp.float32) * n, axis=1, keepdims=True) * softmax_scale
            for q, n in zip(queries, news)
        ]
        positions = lax.broadcasted_iota(jnp.int32, (1, seen), 1)
        masked = [
            jnp.where(positions < len_ref[first + i * STEP + j], scores[j], masked_score)
            for j in every
        ]
        maxima = [
            jnp.maximum(jnp.max(m, axis=1, keepdims=True), n) for m, n in zip(masked, new_scores)
        ]
        probs = [jnp.exp(m - top) for m, top in zip(masked, maxima)]
        new_probs = [jnp.exp(n - top) for n, top in zip(new_scores, maxima)]
        summed = [
            lax.dot_general(
                p.astype(jnp.bfloat16),
                k[:latent],
                (((1,), (1,)), ((), ())),
                preferred_element_type=jnp.float32,
            )
            for p, k in zip(probs, keys)
        ]
        inverse = [
            1.0 / (jnp.sum(p, axis=1, keepdims=True) + n) for p, n in zip(probs, new_probs)
        ]
        for j in every:
            new_low = new_probs[j].astype(jnp.bfloat16).astype(jnp.float32)
            attended = (summed[j] + new_low * news[j][:, :latent]) * inverse[j]
            for c in range(latent // 128):
                stage[c, pl.ds(i * STEP + j, heads, stride=rows), :] = attended[
                    :, c * 128 : (c + 1) * 128
                ]

    longest = len_ref[first + i * STEP]
    for j in range(1, STEP):
        longest = jnp.maximum(longest, len_ref[first + i * STEP + j])
    for seen in range(128, slots + 1, 128):
        in_reach = (longest > seen - 128) & (longest <= seen)
        pl.when(in_reach)(functools.partial(attend_to, seen))

    @pl.when(i == pl.num_programs(0) - 1)
    def _():
        per = heads // (len(outs) * N_CORE)
        for r, out in enumerate(outs):
            for s in range(N_CORE):
                at = pl.multiple_of(group_ref[r * N_CORE + s] * (per * rows), per * rows)
                for c in range(latent // 128):
                    block = stage[c, pl.ds(at, per * rows), :].reshape(per, rows, 128)
                    out[s * per : (s + 1) * per, :, c * 128 : (c + 1) * 128] = block.astype(
                        jnp.bfloat16
                    )


def attend(lengths, groups, queries, cache, new, latent, first, rows):
    reqs, width, heads = queries.shape
    slots = cache.shape[2]
    chips = N_X * N_Y
    at = first // STEP
    block = (heads // chips, rows, latent)
    return pl.pallas_call(
        functools.partial(attend_kernel, first, rows, latent),
        grid_spec=pltpu.PrefetchScalarGridSpec(
            num_scalar_prefetch=2,
            grid=(rows // STEP,),
            in_specs=[
                pl.BlockSpec((STEP, width, heads), lambda i, *_: (at + i, 0, 0)),
                pl.BlockSpec((STEP, width, slots), lambda i, *_: (at + i, 0, 0)),
                pl.BlockSpec((reqs, width), lambda i, *_: (0, 0)),
            ],
            out_specs=[pl.BlockSpec(block, lambda i, *_: (0, 0, 0))] * chips,
            scratch_shapes=[
                pltpu.VMEM((latent // 128, heads * rows, 128), jnp.float32),
                pltpu.VMEM((reqs, width), jnp.float32),
            ],
        ),
        out_shape=[jax.ShapeDtypeStruct(block, jnp.bfloat16)] * chips,
        compiler_params=pltpu.CompilerParams(vmem_limit_bytes=56 << 20),
        cost_estimate=pl.CostEstimate(
            flops=2 * rows * heads * slots * (width + latent),
            bytes_accessed=2 * rows * (width * (slots + heads) + heads * latent),
            transcendentals=rows * heads * slots,
        ),
        name="attend",
    )(lengths, groups, queries, cache, new)


def project_tile(values, own_ref, other_ref):
    half = own_ref.shape[0]
    return jnp.dot(
        values[:, :half], own_ref[...], preferred_element_type=jnp.float32
    ) + jnp.dot(values[:, half:], other_ref[...], preferred_element_type=jnp.float32)


def lift_project_kernel(count, *refs):
    blocks, (own_up, other_up, own_ref, other_ref, values_out, keep, send, values) = (
        refs[:count],
        refs[count:],
    )
    heads = own_up.shape[0]
    depth = own_up.shape[2]

    @pl.when(pl.program_id(0) == 0)
    def _():
        for h in range(2 * heads):
            up = own_up[h] if h < heads else other_up[h - heads]
            rows = jnp.concatenate([b[h] for b in blocks], axis=0)
            lifted = jnp.dot(rows, up, preferred_element_type=jnp.float32).astype(jnp.bfloat16)
            values[:, h * depth : (h + 1) * depth] = lifted
        values_out[...] = values[...]

    tile = project_tile(values[...], own_ref, other_ref).astype(jnp.bfloat16)
    keep[...] = tile[: keep.shape[0]]
    send[...] = tile[keep.shape[0] :]


def lift_project(blocks, own_up, other_up, own, other, start):
    heads, latent, depth = own_up.shape
    rows = sum(b.shape[1] for b in blocks)
    inner, width = own.shape
    steps = (width - start) // TILE
    at = start // TILE
    half = jax.ShapeDtypeStruct((rows // 2, width - start), jnp.bfloat16)
    return pl.pallas_call(
        functools.partial(lift_project_kernel, len(blocks)),
        grid=(steps,),
        in_specs=[pl.BlockSpec(b.shape, lambda i: (0, 0, 0)) for b in blocks]
        + [pl.BlockSpec(own_up.shape, lambda i: (0, 0, 0))] * 2
        + [pl.BlockSpec((inner, TILE), lambda i: (0, at + i))] * 2,
        out_specs=[pl.BlockSpec((rows, 2 * inner), lambda i: (0, 0))]
        + [pl.BlockSpec((rows // 2, TILE), lambda i: (0, i))] * 2,
        out_shape=[jax.ShapeDtypeStruct((rows, 2 * inner), jnp.bfloat16), half, half],
        scratch_shapes=[pltpu.VMEM((rows, 2 * inner), jnp.bfloat16)],
        compiler_params=pltpu.CompilerParams(vmem_limit_bytes=48 << 20),
        cost_estimate=pl.CostEstimate(
            flops=2 * rows * 2 * heads * latent * depth + 4 * rows * inner * (width - start),
            bytes_accessed=4 * inner * (width - start) + 2 * rows * 2 * heads * latent,
            transcendentals=0,
        ),
        name="lift_project",
    )(*blocks, own_up, other_up, own, other)


def project_kernel(values, own_ref, other_ref, *outs):
    tile = project_tile(values[...], own_ref, other_ref).astype(jnp.bfloat16)
    count, (_, rows, _) = len(outs), outs[0].shape
    for dx, out in enumerate(outs):
        for dy in range(N_Y):
            begin = (dy * count + dx) * rows
            out[dy] = tile[begin : begin + rows]


def project(values, own, other, end):
    rows = values.shape[0]
    inner = own.shape[0]
    each = (N_Y, rows // (N_X * N_Y))
    return pl.pallas_call(
        project_kernel,
        grid=(end // TILE,),
        in_specs=[pl.BlockSpec(values.shape, lambda i: (0, 0))]
        + [pl.BlockSpec((inner, TILE), lambda i: (0, i))] * 2,
        out_specs=[pl.BlockSpec((*each, TILE), lambda i: (0, 0, i))] * N_X,
        out_shape=[jax.ShapeDtypeStruct((*each, end), jnp.bfloat16)] * N_X,
        compiler_params=pltpu.CompilerParams(vmem_limit_bytes=48 << 20),
        cost_estimate=pl.CostEstimate(
            flops=4 * rows * inner * end, bytes_accessed=4 * inner * end, transcendentals=0
        ),
        name="project",
    )(values, own, other)


def split_sum_kernel(a_ref, b_ref, *outs):
    rows = outs[0].shape[0]
    for dx, out in enumerate(outs):
        at = slice(dx * rows, (dx + 1) * rows)
        out[...] = (a_ref[at].astype(jnp.float32) + b_ref[at].astype(jnp.float32)).astype(
            jnp.bfloat16
        )


def split_sum(a, b):
    part = jax.ShapeDtypeStruct((a.shape[0] // N_X, a.shape[1]), jnp.bfloat16)
    return pl.pallas_call(
        split_sum_kernel,
        in_specs=[WHOLE] * 2,
        out_specs=[WHOLE] * N_X,
        out_shape=[part] * N_X,
        compiler_params=pltpu.CompilerParams(vmem_limit_bytes=32 << 20),
        name="split_sum",
    )(a, b)


def pair_sum_kernel(a, b, c, d, keep, send):
    for dy, out in enumerate((keep, send)):
        total = a[dy].astype(jnp.float32) + b[dy].astype(jnp.float32)
        total = total + c[dy].astype(jnp.float32) + d[dy].astype(jnp.float32)
        out[...] = total.astype(jnp.bfloat16)


def pair_sum(parts):
    out = jax.ShapeDtypeStruct(parts[0].shape[1:], jnp.bfloat16)
    return pl.pallas_call(
        pair_sum_kernel,
        in_specs=[WHOLE] * len(parts),
        out_specs=[WHOLE] * 2,
        out_shape=[out] * 2,
        compiler_params=pltpu.CompilerParams(vmem_limit_bytes=32 << 20),
        name="pair_sum",
    )(*parts)


def finish_kernel(count, *refs):
    left, right, (residual, gain, hidden, normed) = refs[:2], refs[2:count], refs[count:]
    split = left[0].shape[1]
    squares = 0.0
    for parts, at in ((left, slice(0, split)), (right, slice(split, residual.shape[1]))):
        total = parts[0][...].astype(jnp.float32)
        for part in parts[1:]:
            total = total + part[...].astype(jnp.float32)
        low = (residual[:, at].astype(jnp.float32) + total).astype(jnp.bfloat16)
        hidden[:, at] = low
        wide = low.astype(jnp.float32)
        squares = squares + jnp.sum(wide * wide, axis=1, keepdims=True)
    factor = lax.rsqrt(squares / residual.shape[1] + epsilon)
    normed[...] = (
        hidden[...].astype(jnp.float32) * factor * gain[...].astype(jnp.float32)
    ).astype(jnp.bfloat16)


def finish(left, right, residual, gain):
    out = jax.ShapeDtypeStruct(residual.shape, jnp.bfloat16)
    count = len(left) + len(right)
    return pl.pallas_call(
        functools.partial(finish_kernel, count),
        in_specs=[WHOLE] * (count + 2),
        out_specs=[WHOLE] * 2,
        out_shape=[out] * 2,
        compiler_params=pltpu.CompilerParams(vmem_limit_bytes=32 << 20),
        name="finish",
    )(*left, *right, residual, gain.reshape(1, -1))


def per_device(queries, new_latent, latent_cache, lengths, residual, value_up, out_proj, norm_gain):
    latent = value_up.shape[1]
    reqs = queries.shape[0]
    width = out_proj.shape[1]
    t = lax.axis_index("tp")
    x, y, core = t // (N_Y * N_CORE), t // N_CORE % N_Y, t % N_CORE
    offsets = [(dx, dy) for dy in range(N_Y) for dx in range(N_X)]
    groups = jnp.stack(
        [
            (((x + dx) % N_X) * N_Y + (y ^ dy)) * N_CORE + (core ^ s)
            for dx, dy in offsets
            for s in range(N_CORE)
        ]
    ).astype(jnp.int32)

    other_up = moved(value_up, dcore=1)
    other_proj = moved(out_proj, dcore=1)

    flat_queries = jnp.swapaxes(queries, 1, 2)
    flat_cache = jnp.swapaxes(latent_cache, 1, 2)
    rows = reqs // 2
    order = [(1, 0), (3, 0), (0, 1), (1, 1), (3, 1), (2, 0), (2, 1)]
    arrived = []
    for first in range(0, reqs, rows):
        blocks = attend(
            lengths, groups, flat_queries, flat_cache, new_latent, latent, first, rows
        )
        got = {(0, 0): blocks[0]}
        for dx, dy in order:
            got[dx, dy] = moved(blocks[offsets.index((dx, dy))], dx=dx, dy=dy)
        arrived.append(got)
    blocks = [got[offset] for offset in offsets for got in arrived]

    split = width // 2
    values, keep, send = lift_project(blocks, value_up, other_up, out_proj, other_proj, split)
    y_sum = moved(send, dy=1)
    by_x = project(values, out_proj, other_proj, split)
    left = [by_x[0]] + [moved(by_x[dx], dx=-dx) for dx in (1, 3, 2)]
    right = split_sum(keep, y_sum)
    right = [right[0]] + [moved(right[dx], dx=-dx) for dx in (1, 3, 2)]
    mine, others = pair_sum(left)
    return tuple(finish([mine, moved(others, dy=1)], right, residual, norm_gain))


def solution(mesh):
    return jax.shard_map(
        per_device,
        mesh=mesh,
        in_specs=(
            P(("dp", "tp"), None, None),
            P(("dp", "tp"), None),
            P(("dp", "tp"), None, None),
            P(("dp", "tp")),
            P(("dp", "tp"), None),
            P("tp", None, None),
            P("tp", None),
            P(),
        ),
        out_specs=(P(("dp", "tp"), None), P(("dp", "tp"), None)),
        check_vma=False,
    )
```

```python
import functools

import jax
import jax.numpy as jnp
from jax import lax
from jax.experimental import pallas as pl
from jax.experimental.pallas import tpu as pltpu
from jax.sharding import PartitionSpec as P

softmax_scale = 0.1353
masked_score = -1e30
epsilon = 1e-06

N_X, N_Y, N_CORE = 4, 2, 2
OFFSETS = [(0, 0), (1, 0), (3, 0), (0, 1), (2, 1), (1, 1), (3, 1), (2, 0)]
IN_FLIGHT = 4
STEP = 4
TILE = 1792
WHOLE = pl.BlockSpec(memory_space=pltpu.VMEM)


def moved(array, dx=0, dy=0, dcore=0):
    pairs = []
    for t in range(N_X * N_Y * N_CORE):
        x, y, core = t // (N_Y * N_CORE), t // N_CORE % N_Y, t % N_CORE
        to = ((x + dx) % N_X * N_Y + (y ^ dy)) * N_CORE + (core ^ dcore)
        pairs.append((t, to))
    return lax.ppermute(array, "tp", pairs)


def attend_kernel(first, rows, latent, len_ref, q_ref, c_ref, n_ref, *rest):
    outs, (stage, new_wide) = rest[:-2], rest[-2:]
    i = pl.program_id(0)
    heads, slots = q_ref.shape[2], c_ref.shape[2]

    @pl.when(i == 0)
    def _():
        new_wide[...] = n_ref[...].astype(jnp.float32)

    def attend_to(seen):
        every = range(STEP)
        queries = [q_ref[j].T for j in every]
        keys = [c_ref[j, :, :seen] for j in every]
        news = [new_wide[pl.ds(first + i * STEP + j, 1), :] for j in every]
        scores = [
            jnp.dot(q, k, preferred_element_type=jnp.float32) * softmax_scale
            for q, k in zip(queries, keys)
        ]
        new_scores = [
            jnp.sum(q.astype(jnp.float32) * n, axis=1, keepdims=True) * softmax_scale
            for q, n in zip(queries, news)
        ]
        positions = lax.broadcasted_iota(jnp.int32, (1, seen), 1)
        masked = [
            jnp.where(positions < len_ref[first + i * STEP + j], scores[j], masked_score)
            for j in every
        ]
        maxima = [
            jnp.maximum(jnp.max(m, axis=1, keepdims=True), n) for m, n in zip(masked, new_scores)
        ]
        probs = [jnp.exp(m - top) for m, top in zip(masked, maxima)]
        new_probs = [jnp.exp(n - top) for n, top in zip(new_scores, maxima)]
        summed = [
            lax.dot_general(
                p.astype(jnp.bfloat16),
                k[:latent],
                (((1,), (1,)), ((), ())),
                preferred_element_type=jnp.float32,
            )
            for p, k in zip(probs, keys)
        ]
        inverse = [
            1.0 / (jnp.sum(p, axis=1, keepdims=True) + n) for p, n in zip(probs, new_probs)
        ]
        for j in every:
            new_low = new_probs[j].astype(jnp.bfloat16).astype(jnp.float32)
            attended = (summed[j] + new_low * news[j][:, :latent]) * inverse[j]
            for c in range(latent // 128):
                stage[c, pl.ds(i * STEP + j, heads, stride=rows), :] = attended[
                    :, c * 128 : (c + 1) * 128
                ]

    longest = len_ref[first + i * STEP]
    for j in range(1, STEP):
        longest = jnp.maximum(longest, len_ref[first + i * STEP + j])
    for seen in range(128, slots + 1, 128):
        in_reach = (longest > seen - 128) & (longest <= seen)
        pl.when(in_reach)(functools.partial(attend_to, seen))

    @pl.when(i == pl.num_programs(0) - 1)
    def _():
        per = heads // (len(outs) * N_CORE)
        t = lax.axis_index("tp")
        x, y, core = t // (N_Y * N_CORE), t // N_CORE % N_Y, t % N_CORE
        for (dx, dy), out in zip(OFFSETS, outs):
            chip = (x + dx) % N_X * N_Y + (y ^ dy)
            for s in range(N_CORE):
                at = pl.multiple_of((chip * N_CORE + (core ^ s)) * (per * rows), per * rows)
                for c in range(latent // 128):
                    block = stage[c, pl.ds(at, per * rows), :].reshape(per, rows, 128)
                    out[s * per : (s + 1) * per, :, c * 128 : (c + 1) * 128] = block.astype(
                        jnp.bfloat16
                    )


def attend(lengths, queries, cache, new, latent, first, rows):
    reqs, width, heads = queries.shape
    slots = cache.shape[2]
    chips = N_X * N_Y
    at = first // STEP
    block = (heads // chips, rows, latent)
    return pl.pallas_call(
        functools.partial(attend_kernel, first, rows, latent),
        grid_spec=pltpu.PrefetchScalarGridSpec(
            num_scalar_prefetch=1,
            grid=(rows // STEP,),
            in_specs=[
                pl.BlockSpec((STEP, width, heads), lambda i, *_: (at + i, 0, 0)),
                pl.BlockSpec((STEP, width, slots), lambda i, *_: (at + i, 0, 0)),
                pl.BlockSpec((reqs, width), lambda i, *_: (0, 0)),
            ],
            out_specs=[pl.BlockSpec(block, lambda i, *_: (0, 0, 0))] * chips,
            scratch_shapes=[
                pltpu.VMEM((latent // 128, heads * rows, 128), jnp.float32),
                pltpu.VMEM((reqs, width), jnp.float32),
            ],
        ),
        out_shape=[jax.ShapeDtypeStruct(block, jnp.bfloat16)] * chips,
        compiler_params=pltpu.CompilerParams(vmem_limit_bytes=20 << 20),
        cost_estimate=pl.CostEstimate(
            flops=8 * rows * heads * slots * (width + latent),
            bytes_accessed=2 * rows * (width * (slots + heads) + heads * latent),
            transcendentals=rows * heads * slots,
        ),
        name="attend",
    )(lengths, queries, cache, new)


def lift_kernel(count, *refs):
    blocks, (own_up, other_up, *earlier, values) = refs[:count], refs[count:]
    heads, _, depth = own_up.shape
    rows = blocks[0].shape[1]
    blocks = [blocks[OFFSETS.index((dx, dy))] for dy in range(N_Y) for dx in range(N_X)]
    for h in range(2 * heads):
        up = own_up[h] if h < heads else other_up[h - heads]
        stacked = jnp.concatenate([b[h] for b in blocks], axis=0)
        lifted = jnp.dot(stacked, up, preferred_element_type=jnp.float32).astype(jnp.bfloat16)
        at = slice(h * depth, (h + 1) * depth)
        if not earlier:
            values[:, at] = lifted
            continue
        for n in range(count):
            here = slice(n * rows, (n + 1) * rows)
            values[2 * n * rows : (2 * n + 1) * rows, at] = earlier[0][here, at]
            values[(2 * n + 1) * rows : (2 * n + 2) * rows, at] = lifted[here]


def lift(blocks, own_up, other_up, *earlier):
    heads, latent, depth = own_up.shape
    rows = sum(b.shape[1] for b in blocks)
    return pl.pallas_call(
        functools.partial(lift_kernel, len(blocks)),
        in_specs=[WHOLE] * (len(blocks) + 2 + len(earlier)),
        out_specs=WHOLE,
        out_shape=jax.ShapeDtypeStruct((rows * (1 + len(earlier)), 2 * heads * depth), jnp.bfloat16),
        compiler_params=pltpu.CompilerParams(vmem_limit_bytes=16 << 20),
        cost_estimate=pl.CostEstimate(
            flops=8 * rows * heads * latent * depth,
            bytes_accessed=4 * rows * heads * latent,
            transcendentals=0,
        ),
        name="lift",
    )(*blocks, own_up, other_up, *earlier)


def project_kernel(start, split, values, own_ref, other_ref, *outs):
    inner = own_ref.shape[0]
    at = pl.ds(pl.multiple_of(start + pl.program_id(0) * TILE, TILE), TILE)
    tile = jnp.dot(values[:, :inner], own_ref[:, at], preferred_element_type=jnp.float32)
    tile = tile + jnp.dot(values[:, inner:], other_ref[:, at], preferred_element_type=jnp.float32)
    tile = tile.astype(jnp.bfloat16)
    if split == "y":
        rows = tile.shape[0] // N_Y
        for dy, out in enumerate(outs):
            out[...] = tile[dy * rows : (dy + 1) * rows]
        return
    rows = tile.shape[0] // (N_X * N_Y)
    for dx, out in enumerate(outs):
        for dy in range(N_Y):
            begin = (dy * N_X + dx) * rows
            out[dy] = tile[begin : begin + rows]


def project(values, own, other, start, end, split):
    rows = values.shape[0]
    inner = own.shape[0]
    each, index, count = (rows // N_Y,), lambda i: (0, i), N_Y
    if split == "x":
        each, index, count = (N_Y, rows // (N_X * N_Y)), lambda i: (0, 0, i), N_X
    own, other = (pltpu.with_memory_space_constraint(w, pltpu.VMEM) for w in (own, other))
    return pl.pallas_call(
        functools.partial(project_kernel, start, split),
        grid=((end - start) // TILE,),
        in_specs=[WHOLE] * 3,
        out_specs=[pl.BlockSpec((*each, TILE), index)] * count,
        out_shape=[jax.ShapeDtypeStruct((*each, end - start), jnp.bfloat16)] * count,
        compiler_params=pltpu.CompilerParams(vmem_limit_bytes=12 << 20),
        cost_estimate=pl.CostEstimate(
            flops=4 * rows * inner * (end - start),
            bytes_accessed=2 * rows * (end - start),
            transcendentals=0,
        ),
        name="project",
    )(values, own, other)


def split_sum_kernel(a_ref, b_ref, *outs):
    rows = outs[0].shape[0]
    for dx, out in enumerate(outs):
        at = slice(dx * rows, (dx + 1) * rows)
        out[...] = (a_ref[at].astype(jnp.float32) + b_ref[at].astype(jnp.float32)).astype(
            jnp.bfloat16
        )


def split_sum(a, b):
    part = jax.ShapeDtypeStruct((a.shape[0] // N_X, a.shape[1]), jnp.bfloat16)
    return pl.pallas_call(
        split_sum_kernel,
        in_specs=[WHOLE] * 2,
        out_specs=[WHOLE] * N_X,
        out_shape=[part] * N_X,
        compiler_params=pltpu.CompilerParams(vmem_limit_bytes=32 << 20),
        name="split_sum",
    )(a, b)


def pair_sum_kernel(a, b, c, d, keep, send):
    for dy, out in enumerate((keep, send)):
        total = a[dy].astype(jnp.float32) + b[dy].astype(jnp.float32)
        total = total + c[dy].astype(jnp.float32) + d[dy].astype(jnp.float32)
        out[...] = total.astype(jnp.bfloat16)


def pair_sum(parts):
    out = jax.ShapeDtypeStruct(parts[0].shape[1:], jnp.bfloat16)
    return pl.pallas_call(
        pair_sum_kernel,
        in_specs=[WHOLE] * len(parts),
        out_specs=[WHOLE] * 2,
        out_shape=[out] * 2,
        compiler_params=pltpu.CompilerParams(vmem_limit_bytes=32 << 20),
        name="pair_sum",
    )(*parts)


def finish_kernel(count, *refs):
    left, right, (residual, gain, hidden, normed) = refs[:2], refs[2:count], refs[count:]
    split = left[0].shape[1]
    squares = 0.0
    for parts, at in ((left, slice(0, split)), (right, slice(split, residual.shape[1]))):
        total = parts[0][...].astype(jnp.float32)
        for part in parts[1:]:
            total = total + part[...].astype(jnp.float32)
        low = (residual[:, at].astype(jnp.float32) + total).astype(jnp.bfloat16)
        hidden[:, at] = low
        wide = low.astype(jnp.float32)
        squares = squares + jnp.sum(wide * wide, axis=1, keepdims=True)
    factor = lax.rsqrt(squares / residual.shape[1] + epsilon)
    normed[...] = (
        hidden[...].astype(jnp.float32) * factor * gain[...].astype(jnp.float32)
    ).astype(jnp.bfloat16)


def finish(left, right, residual, gain):
    out = jax.ShapeDtypeStruct(residual.shape, jnp.bfloat16)
    count = len(left) + len(right)
    return pl.pallas_call(
        functools.partial(finish_kernel, count),
        in_specs=[WHOLE] * (count + 2),
        out_specs=[WHOLE] * 2,
        out_shape=[out] * 2,
        compiler_params=pltpu.CompilerParams(vmem_limit_bytes=32 << 20),
        name="finish",
    )(*left, *right, residual, gain.reshape(1, -1))


def per_device(queries, new_latent, latent_cache, lengths, residual, value_up, out_proj, norm_gain):
    latent = value_up.shape[1]
    reqs = queries.shape[0]
    width = out_proj.shape[1]
    other_up = moved(value_up, dcore=1)
    other_proj = moved(out_proj, dcore=1)

    flat_queries, flat_cache = (
        pltpu.with_memory_space_constraint(jnp.swapaxes(a, 1, 2), pltpu.HBM)
        for a in (queries, latent_cache)
    )
    rows = reqs // 2
    values, going = [], []
    for first in range(0, reqs, rows):
        blocks = attend(lengths, flat_queries, flat_cache, new_latent, latent, first, rows)
        got = [blocks[0]]
        for (dx, dy), block in zip(OFFSETS[1:], blocks[1:]):
            if len(going) >= IN_FLIGHT:
                block, _ = lax.optimization_barrier((block, going[-IN_FLIGHT]))
            got.append(moved(block, dx=dx, dy=dy))
            going.append(got[-1])
        values = [lift(got, value_up, other_up, *values)]

    half = width // 2
    keep, send = project(values[0], out_proj, other_proj, half, width, "y")
    y_sum = moved(send, dy=1)
    by_x = project(values[0], out_proj, other_proj, 0, half, "x")
    left = [by_x[0]] + [moved(by_x[dx], dx=-dx) for dx in (1, 3, 2)]
    right = split_sum(keep, y_sum)
    right = [right[0]] + [moved(right[dx], dx=-dx) for dx in (1, 3, 2)]
    mine, others = pair_sum(left)
    return tuple(finish([mine, moved(others, dy=1)], right, residual, norm_gain))


def solution(mesh):
    return jax.shard_map(
        per_device,
        mesh=mesh,
        in_specs=(
            P(("dp", "tp"), None, None),
            P(("dp", "tp"), None),
            P(("dp", "tp"), None, None),
            P(("dp", "tp")),
            P(("dp", "tp"), None),
            P("tp", None, None),
            P("tp", None),
            P(),
        ),
        out_specs=(P(("dp", "tp"), None), P(("dp", "tp"), None)),
        check_vma=False,
    )
```

```python
import functools

import jax
import jax.numpy as jnp
from jax import lax
from jax.experimental import pallas as pl
from jax.experimental.pallas import tpu as pltpu
from jax.sharding import PartitionSpec as P

softmax_scale = 0.1353
masked_score = -1e30
epsilon = 1e-06

N_X, N_Y, N_CORE = 4, 2, 2
STEP = 4
FLUSH = 16
STEPS = 2
WHOLE = pl.BlockSpec(memory_space=pltpu.VMEM)


def moved(array, dx=0, dy=0, dcore=0):
    pairs = []
    for t in range(N_X * N_Y * N_CORE):
        x, y, core = t // (N_Y * N_CORE), t // N_CORE % N_Y, t % N_CORE
        to = ((x + dx) % N_X * N_Y + (y ^ dy)) * N_CORE + (core ^ dcore)
        pairs.append((t, to))
    return lax.ppermute(array, "tp", pairs)


def attend_kernel(latent, len_ref, q_ref, c_ref, n_ref, *rest):
    outs, (stage, new_wide) = rest[:-2], rest[-2:]
    i = pl.program_id(0)
    heads, slots = q_ref.shape[2], c_ref.shape[2]
    rows = n_ref.shape[0]

    @pl.when(i == 0)
    def _():
        new_wide[...] = n_ref[...].astype(jnp.float32)

    def attend_to(seen):
        every = range(STEP)
        queries = [q_ref[j].T for j in every]
        keys = [c_ref[j, :, :seen] for j in every]
        news = [new_wide[pl.ds(i * STEP + j, 1), :] for j in every]
        scores = [
            jnp.dot(q, k, preferred_element_type=jnp.float32) * softmax_scale
            for q, k in zip(queries, keys)
        ]
        new_scores = [
            jnp.sum(q.astype(jnp.float32) * n, axis=1, keepdims=True) * softmax_scale
            for q, n in zip(queries, news)
        ]
        positions = lax.broadcasted_iota(jnp.int32, (1, seen), 1)
        masked = [
            jnp.where(positions < len_ref[i * STEP + j], scores[j], masked_score)
            for j in every
        ]
        maxima = [
            jnp.maximum(jnp.max(m, axis=1, keepdims=True), n) for m, n in zip(masked, new_scores)
        ]
        probs = [jnp.exp(m - top) for m, top in zip(masked, maxima)]
        new_probs = [jnp.exp(n - top) for n, top in zip(new_scores, maxima)]
        summed = [
            lax.dot_general(
                p.astype(jnp.bfloat16),
                k[:latent],
                (((1,), (1,)), ((), ())),
                preferred_element_type=jnp.float32,
            )
            for p, k in zip(probs, keys)
        ]
        inverse = [
            1.0 / (jnp.sum(p, axis=1, keepdims=True) + n) for p, n in zip(probs, new_probs)
        ]
        for j in every:
            new_low = new_probs[j].astype(jnp.bfloat16).astype(jnp.float32)
            attended = (summed[j] + new_low * news[j][:, :latent]) * inverse[j]
            for c in range(latent // 128):
                stage[c, pl.ds(i % (FLUSH // STEP) * STEP + j, heads, stride=FLUSH), :] = attended[
                    :, c * 128 : (c + 1) * 128
                ]

    longest = len_ref[i * STEP]
    for j in range(1, STEP):
        longest = jnp.maximum(longest, len_ref[i * STEP + j])
    for seen in range(128, slots + 1, 128):
        in_reach = (longest > seen - 128) & (longest <= seen)
        pl.when(in_reach)(functools.partial(attend_to, seen))

    def flush(begin):
        per = heads // (N_X * N_Y * N_CORE)
        t = lax.axis_index("tp")
        x, y, core = t // (N_Y * N_CORE), t // N_CORE % N_Y, t % N_CORE
        for dx in range(N_X):
            for dy in range(N_Y):
                chip = (x + dx) % N_X * N_Y + (y ^ dy)
                for out, to in ((outs[dx].at[dy], core), (outs[N_X + dy].at[dx], core ^ 1)):
                    at = pl.multiple_of((chip * N_CORE + to) * (per * FLUSH), per * FLUSH)
                    for c in range(latent // 128):
                        block = stage[c, pl.ds(at, per * FLUSH), :].reshape(per, FLUSH, 128)
                        out[:, begin : begin + FLUSH, c * 128 : (c + 1) * 128] = block.astype(
                            jnp.bfloat16
                        )

    for begin in range(0, rows, FLUSH):
        pl.when((i + 1) * STEP == begin + FLUSH)(functools.partial(flush, begin))


def attend(lengths, queries, cache, new, latent):
    rows, width, heads = queries.shape
    slots = cache.shape[2]
    block = (heads // (N_X * N_Y * N_CORE), rows, latent)
    shapes = [(N_Y, *block)] * N_X + [(N_X, *block)] * N_Y
    return pl.pallas_call(
        functools.partial(attend_kernel, latent),
        grid_spec=pltpu.PrefetchScalarGridSpec(
            num_scalar_prefetch=1,
            grid=(rows // STEP,),
            in_specs=[
                pl.BlockSpec((STEP, width, heads), lambda i, *_: (i, 0, 0)),
                pl.BlockSpec((STEP, width, slots), lambda i, *_: (i, 0, 0)),
                pl.BlockSpec((rows, width), lambda i, *_: (0, 0)),
            ],
            out_specs=[pl.BlockSpec(shape, lambda i, *_: (0, 0, 0, 0)) for shape in shapes],
            scratch_shapes=[
                pltpu.VMEM((latent // 128, heads * FLUSH, 128), jnp.float32),
                pltpu.VMEM((rows, width), jnp.float32),
            ],
        ),
        out_shape=[jax.ShapeDtypeStruct(shape, jnp.bfloat16) for shape in shapes],
        compiler_params=pltpu.CompilerParams(vmem_limit_bytes=18 << 20),
        cost_estimate=pl.CostEstimate(
            flops=8 * rows * heads * slots * (width + latent),
            bytes_accessed=2 * rows * (width * (slots + heads) + heads * latent),
            transcendentals=rows * heads * slots,
        ),
        name="attend",
    )(lengths, queries, cache, new)


def regroup_kernel(count, picks, *refs):
    ins, outs = refs[:count], refs[count:]
    for out, pick in zip(outs, picks):
        for to, (n, at) in enumerate(pick):
            out[to] = ins[n][at]


def regroup(arrays, picks):
    block = arrays[0].shape[1:]
    return pl.pallas_call(
        functools.partial(regroup_kernel, len(arrays), picks),
        in_specs=[WHOLE] * len(arrays),
        out_specs=[WHOLE] * len(picks),
        out_shape=[jax.ShapeDtypeStruct((len(p), *block), jnp.bfloat16) for p in picks],
        compiler_params=pltpu.CompilerParams(vmem_limit_bytes=8 << 20),
        name="regroup",
    )(*arrays)


def lift_kernel(count, picks, *refs):
    arrays, (own_up, other_up, values) = refs[:count], refs[count:]
    heads, _, depth = own_up.shape
    for s, up in enumerate((own_up, other_up)):
        for h in range(heads):
            rows = jnp.concatenate([arrays[n][at, h] for n, at in picks[s]], axis=0)
            lifted = jnp.dot(rows, up[h], preferred_element_type=jnp.float32)
            at = (s * heads + h) * depth
            values[:, at : at + depth] = lifted.astype(jnp.bfloat16)


def lift(arrays, picks, own_up, other_up):
    heads, latent, depth = own_up.shape
    rows = len(picks[0]) * arrays[0].shape[2]
    return pl.pallas_call(
        functools.partial(lift_kernel, len(arrays), picks),
        in_specs=[WHOLE] * (len(arrays) + 2),
        out_specs=WHOLE,
        out_shape=jax.ShapeDtypeStruct((rows, N_CORE * heads * depth), jnp.bfloat16),
        compiler_params=pltpu.CompilerParams(vmem_limit_bytes=10 << 20),
        cost_estimate=pl.CostEstimate(
            flops=4 * rows * heads * latent * depth,
            bytes_accessed=4 * rows * heads * latent,
            transcendentals=0,
        ),
        name="lift",
    )(*arrays, own_up, other_up)


def project_kernel(start, split, values, own_ref, other_ref, *outs):
    inner, width = own_ref.shape[0], outs[0].shape[-1]
    at = pl.ds(pl.multiple_of(start + pl.program_id(0) * width, 128), width)
    tile = jnp.dot(values[:, :inner], own_ref[:, at], preferred_element_type=jnp.float32)
    tile = tile + jnp.dot(values[:, inner:], other_ref[:, at], preferred_element_type=jnp.float32)
    tile = tile.astype(jnp.bfloat16)
    if split == "y":
        begin = 0
        for out in outs:
            out[...] = tile[begin : begin + out.shape[0]]
            begin += out.shape[0]
        return
    rows = tile.shape[0] // (N_X * N_Y)
    for dx, out in enumerate(outs):
        for dy in range(N_Y):
            begin = (dy * N_X + dx) * rows
            out[dy] = tile[begin : begin + rows]


def project(values, own, other, start, end, split):
    rows = values.shape[0]
    inner = own.shape[0]
    blocks, index = [(rows // 2,), (rows // 4,), (rows // 4,)], lambda i: (0, i)
    if split == "x":
        blocks, index = [(N_Y, rows // (N_X * N_Y))] * N_X, lambda i: (0, 0, i)
    own, other = (pltpu.with_memory_space_constraint(w, pltpu.VMEM) for w in (own, other))
    return pl.pallas_call(
        functools.partial(project_kernel, start, split),
        grid=(STEPS,),
        in_specs=[WHOLE] * 3,
        out_specs=[pl.BlockSpec((*b, (end - start) // STEPS), index) for b in blocks],
        out_shape=[jax.ShapeDtypeStruct((*b, end - start), jnp.bfloat16) for b in blocks],
        compiler_params=pltpu.CompilerParams(vmem_limit_bytes=18 << 20),
        cost_estimate=pl.CostEstimate(
            flops=4 * rows * inner * (end - start),
            bytes_accessed=2 * rows * (end - start),
            transcendentals=0,
        ),
        name="project",
    )(values, own, other)


def split_sum_kernel(a_ref, b_ref, c_ref, *outs):
    rows = outs[0].shape[0]
    for dx, out in enumerate(outs):
        ref, at = (b_ref, dx) if dx < N_X // 2 else (c_ref, dx - N_X // 2)
        low = ref[at * rows : (at + 1) * rows].astype(jnp.float32)
        out[...] = (a_ref[dx * rows : (dx + 1) * rows].astype(jnp.float32) + low).astype(
            jnp.bfloat16
        )


def split_sum(a, b, c):
    part = jax.ShapeDtypeStruct((a.shape[0] // N_X, a.shape[1]), jnp.bfloat16)
    return pl.pallas_call(
        split_sum_kernel,
        in_specs=[WHOLE] * 3,
        out_specs=[WHOLE] * N_X,
        out_shape=[part] * N_X,
        compiler_params=pltpu.CompilerParams(vmem_limit_bytes=8 << 20),
        name="split_sum",
    )(a, b, c)


def pair_sum_kernel(a, b, c, d, keep, send):
    for dy, out in enumerate((keep, send)):
        total = a[dy].astype(jnp.float32) + b[dy].astype(jnp.float32)
        total = total + c[dy].astype(jnp.float32) + d[dy].astype(jnp.float32)
        out[...] = total.astype(jnp.bfloat16)


def pair_sum(parts):
    out = jax.ShapeDtypeStruct(parts[0].shape[1:], jnp.bfloat16)
    return pl.pallas_call(
        pair_sum_kernel,
        in_specs=[WHOLE] * len(parts),
        out_specs=[WHOLE] * 2,
        out_shape=[out] * 2,
        compiler_params=pltpu.CompilerParams(vmem_limit_bytes=8 << 20),
        name="pair_sum",
    )(*parts)


def finish_kernel(count, *refs):
    left, right, (residual, gain, hidden, normed) = refs[:2], refs[2:count], refs[count:]
    split = left[0].shape[1]
    squares = 0.0
    for parts, at in ((left, slice(0, split)), (right, slice(split, residual.shape[1]))):
        total = parts[0][...].astype(jnp.float32)
        for part in parts[1:]:
            total = total + part[...].astype(jnp.float32)
        low = (residual[:, at].astype(jnp.float32) + total).astype(jnp.bfloat16)
        hidden[:, at] = low
        wide = low.astype(jnp.float32)
        squares = squares + jnp.sum(wide * wide, axis=1, keepdims=True)
    factor = lax.rsqrt(squares / residual.shape[1] + epsilon)
    normed[...] = (
        hidden[...].astype(jnp.float32) * factor * gain[...].astype(jnp.float32)
    ).astype(jnp.bfloat16)


def finish(left, right, residual, gain):
    out = jax.ShapeDtypeStruct(residual.shape, jnp.bfloat16)
    count = len(left) + len(right)
    return pl.pallas_call(
        functools.partial(finish_kernel, count),
        in_specs=[WHOLE] * (count + 2),
        out_specs=[WHOLE] * 2,
        out_shape=[out] * 2,
        compiler_params=pltpu.CompilerParams(vmem_limit_bytes=8 << 20),
        name="finish",
    )(*left, *right, residual, gain.reshape(1, -1))


def per_device(queries, new_latent, latent_cache, lengths, residual, value_up, out_proj, norm_gain):
    latent = value_up.shape[1]
    width = out_proj.shape[1]
    flat_queries, flat_cache = (
        pltpu.with_memory_space_constraint(jnp.swapaxes(a, 1, 2), pltpu.HBM)
        for a in (queries, latent_cache)
    )
    new_latent = pltpu.with_memory_space_constraint(new_latent, pltpu.HBM)
    lengths = pltpu.with_memory_space_constraint(lengths, pltpu.HBM)
    other_proj = moved(out_proj, dcore=1)
    other_up = moved(value_up, dcore=1)
    blocks = list(attend(lengths, flat_queries, flat_cache, new_latent, latent))
    blocks[N_X - 1], _ = lax.optimization_barrier((blocks[N_X - 1], other_up))

    by_y = [blocks[N_X], moved(blocks[N_X + 1], dy=1)]
    by_x = [blocks[0]] + [moved(blocks[dx], dx=dx) for dx in range(1, N_X)]
    spread = regroup(by_y, [[(dy, dx) for dy in range(N_Y)] for dx in range(1, N_X)])
    spread = [moved(spread[dx - 1], dx=dx) for dx in range(1, N_X)]
    (crossed,) = regroup(by_x, [[(dx, 1) for dx in range(N_X)]])
    crossed = moved(crossed, dy=1)

    arrays = [*by_x, crossed, *by_y, *spread]
    own = [(dx, 0) for dx in range(N_X)] + [(N_X, dx) for dx in range(N_X)]
    other = []
    for dy in range(N_Y):
        other.append((N_X + 1 + dy, 0))
        other += [(N_X + 1 + N_Y + dx - 1, dy) for dx in range(1, N_X)]
    values = lift(arrays, (own, other), value_up, other_up)

    split = width * 4 // 7
    sums = project(values, out_proj, other_proj, 0, split, "x")
    left = [sums[0]] + [moved(sums[dx], dx=-dx) for dx in (1, 3, 2)]
    values, _ = lax.optimization_barrier((values, sums[0]))
    keep, *send = project(values, out_proj, other_proj, split, width, "y")
    right = split_sum(keep, *(moved(s, dy=1) for s in send))
    right = [right[0]] + [moved(right[dx], dx=-dx) for dx in (1, 3, 2)]
    mine, others = pair_sum(left)
    return tuple(finish([mine, moved(others, dy=1)], right, residual, norm_gain))


def solution(mesh):
    return jax.shard_map(
        per_device,
        mesh=mesh,
        in_specs=(
            P(("dp", "tp"), None, None),
            P(("dp", "tp"), None),
            P(("dp", "tp"), None, None),
            P(("dp", "tp")),
            P(("dp", "tp"), None),
            P("tp", None, None),
            P("tp", None),
            P(),
        ),
        out_specs=(P(("dp", "tp"), None), P(("dp", "tp"), None)),
        check_vma=False,
    )
```

```python
import functools

import jax
import jax.numpy as jnp
from jax import lax
from jax.experimental import pallas as pl
from jax.experimental.pallas import tpu as pltpu
from jax.sharding import PartitionSpec as P

softmax_scale = 0.1353
masked_score = -1e30
epsilon = 1e-06

N_X, N_Y, N_CORE = 4, 2, 2
STEP = 4
FLUSH = 16
STEPS = 2
WHOLE = pl.BlockSpec(memory_space=pltpu.VMEM)


def moved(array, dx=0, dy=0, dcore=0):
    pairs = []
    for t in range(N_X * N_Y * N_CORE):
        x, y, core = t // (N_Y * N_CORE), t // N_CORE % N_Y, t % N_CORE
        to = ((x + dx) % N_X * N_Y + (y ^ dy)) * N_CORE + (core ^ dcore)
        pairs.append((t, to))
    return lax.ppermute(array, "tp", pairs)


def attend_kernel(latent, len_ref, q_ref, c_ref, n_ref, *rest):
    outs, (stage, new_wide) = rest[:-2], rest[-2:]
    i = pl.program_id(0)
    heads, slots = q_ref.shape[2], c_ref.shape[2]
    rows = n_ref.shape[0]

    @pl.when(i == 0)
    def _():
        new_wide[...] = n_ref[...].astype(jnp.float32)

    def attend_to(seen):
        every = range(STEP)
        queries = [q_ref[j].T for j in every]
        keys = [c_ref[j, :, :seen] for j in every]
        news = [new_wide[pl.ds(i * STEP + j, 1), :] for j in every]
        scores = [
            jnp.dot(q, k, preferred_element_type=jnp.float32) * softmax_scale
            for q, k in zip(queries, keys)
        ]
        new_scores = [
            jnp.sum(q.astype(jnp.float32) * n, axis=1, keepdims=True) * softmax_scale
            for q, n in zip(queries, news)
        ]
        positions = lax.broadcasted_iota(jnp.int32, (1, seen), 1)
        masked = [
            jnp.where(positions < len_ref[i * STEP + j], scores[j], masked_score)
            for j in every
        ]
        maxima = [
            jnp.maximum(jnp.max(m, axis=1, keepdims=True), n) for m, n in zip(masked, new_scores)
        ]
        probs = [jnp.exp(m - top) for m, top in zip(masked, maxima)]
        new_probs = [jnp.exp(n - top) for n, top in zip(new_scores, maxima)]
        summed = [
            lax.dot_general(
                p.astype(jnp.bfloat16),
                k[:latent],
                (((1,), (1,)), ((), ())),
                preferred_element_type=jnp.float32,
            )
            for p, k in zip(probs, keys)
        ]
        inverse = [
            1.0 / (jnp.sum(p, axis=1, keepdims=True) + n) for p, n in zip(probs, new_probs)
        ]
        for j in every:
            new_low = new_probs[j].astype(jnp.bfloat16).astype(jnp.float32)
            attended = (summed[j] + new_low * news[j][:, :latent]) * inverse[j]
            for c in range(latent // 128):
                stage[c, pl.ds(i % (FLUSH // STEP) * STEP + j, heads, stride=FLUSH), :] = attended[
                    :, c * 128 : (c + 1) * 128
                ]

    longest = len_ref[i * STEP]
    for j in range(1, STEP):
        longest = jnp.maximum(longest, len_ref[i * STEP + j])
    for seen in range(128, slots + 1, 128):
        in_reach = (longest > seen - 128) & (longest <= seen)
        pl.when(in_reach)(functools.partial(attend_to, seen))

    def flush(begin):
        per = heads // (N_X * N_Y * N_CORE)
        t = lax.axis_index("tp")
        x, y, core = t // (N_Y * N_CORE), t // N_CORE % N_Y, t % N_CORE
        for dx in range(N_X):
            for dy in range(N_Y):
                chip = (x + dx) % N_X * N_Y + (y ^ dy)
                for out, to in ((outs[dx].at[dy], core), (outs[N_X + dy].at[dx], core ^ 1)):
                    at = pl.multiple_of((chip * N_CORE + to) * (per * FLUSH), per * FLUSH)
                    for c in range(latent // 128):
                        block = stage[c, pl.ds(at, per * FLUSH), :].reshape(per, FLUSH, 128)
                        out[:, begin : begin + FLUSH, c * 128 : (c + 1) * 128] = block.astype(
                            jnp.bfloat16
                        )

    for begin in range(0, rows, FLUSH):
        pl.when((i + 1) * STEP == begin + FLUSH)(functools.partial(flush, begin))


def attend(lengths, queries, cache, new, latent):
    rows, width, heads = queries.shape
    slots = cache.shape[2]
    block = (heads // (N_X * N_Y * N_CORE), rows, latent)
    shapes = [(N_Y, *block)] * N_X + [(N_X, *block)] * N_Y
    return pl.pallas_call(
        functools.partial(attend_kernel, latent),
        grid_spec=pltpu.PrefetchScalarGridSpec(
            num_scalar_prefetch=1,
            grid=(rows // STEP,),
            in_specs=[
                pl.BlockSpec((STEP, width, heads), lambda i, *_: (i, 0, 0)),
                pl.BlockSpec((STEP, width, slots), lambda i, *_: (i, 0, 0)),
                pl.BlockSpec((rows, width), lambda i, *_: (0, 0)),
            ],
            out_specs=[pl.BlockSpec(shape, lambda i, *_: (0, 0, 0, 0)) for shape in shapes],
            scratch_shapes=[
                pltpu.VMEM((latent // 128, heads * FLUSH, 128), jnp.float32),
                pltpu.VMEM((rows, width), jnp.float32),
            ],
        ),
        out_shape=[jax.ShapeDtypeStruct(shape, jnp.bfloat16) for shape in shapes],
        compiler_params=pltpu.CompilerParams(vmem_limit_bytes=18 << 20),
        cost_estimate=pl.CostEstimate(
            flops=8 * rows * heads * slots * (width + latent),
            bytes_accessed=2 * rows * (width * (slots + heads) + heads * latent),
            transcendentals=rows * heads * slots,
        ),
        name="attend",
    )(lengths, queries, cache, new)


def regroup_kernel(count, picks, *refs):
    ins, outs = refs[:count], refs[count:]
    for out, pick in zip(outs, picks):
        for to, (n, at) in enumerate(pick):
            out[to] = ins[n][at]


def regroup(arrays, picks):
    block = arrays[0].shape[1:]
    return pl.pallas_call(
        functools.partial(regroup_kernel, len(arrays), picks),
        in_specs=[WHOLE] * len(arrays),
        out_specs=[WHOLE] * len(picks),
        out_shape=[jax.ShapeDtypeStruct((len(p), *block), jnp.bfloat16) for p in picks],
        compiler_params=pltpu.CompilerParams(vmem_limit_bytes=8 << 20),
        name="regroup",
    )(*arrays)


def lift_kernel(count, picks, *refs):
    arrays, (own_up, other_up, values) = refs[:count], refs[count:]
    heads, _, depth = own_up.shape
    for s, up in enumerate((own_up, other_up)):
        for h in range(heads):
            rows = jnp.concatenate([arrays[n][at, h] for n, at in picks[s]], axis=0)
            lifted = jnp.dot(rows, up[h], preferred_element_type=jnp.float32)
            at = (s * heads + h) * depth
            values[:, at : at + depth] = lifted.astype(jnp.bfloat16)


def lift(arrays, picks, own_up, other_up):
    heads, latent, depth = own_up.shape
    rows = len(picks[0]) * arrays[0].shape[2]
    return pl.pallas_call(
        functools.partial(lift_kernel, len(arrays), picks),
        in_specs=[WHOLE] * (len(arrays) + 2),
        out_specs=WHOLE,
        out_shape=jax.ShapeDtypeStruct((rows, N_CORE * heads * depth), jnp.bfloat16),
        compiler_params=pltpu.CompilerParams(vmem_limit_bytes=10 << 20),
        cost_estimate=pl.CostEstimate(
            flops=4 * rows * heads * latent * depth,
            bytes_accessed=4 * rows * heads * latent,
            transcendentals=0,
        ),
        name="lift",
    )(*arrays, own_up, other_up)


def project_kernel(start, split, values, own_ref, other_ref, *outs):
    inner, width = own_ref.shape[0], outs[0].shape[-1]
    at = pl.ds(pl.multiple_of(start + pl.program_id(0) * width, 128), width)
    tile = jnp.dot(values[:, :inner], own_ref[:, at], preferred_element_type=jnp.float32)
    tile = tile + jnp.dot(values[:, inner:], other_ref[:, at], preferred_element_type=jnp.float32)
    tile = tile.astype(jnp.bfloat16)
    if split == "y":
        begin = 0
        for out in outs:
            out[...] = tile[begin : begin + out.shape[0]]
            begin += out.shape[0]
        return
    rows = tile.shape[0] // (N_X * N_Y)
    for dx, out in enumerate(outs):
        for dy in range(N_Y):
            begin = (dy * N_X + dx) * rows
            out[dy] = tile[begin : begin + rows]


def project(values, own, other, start, end, split):
    rows = values.shape[0]
    inner = own.shape[0]
    blocks, index = [(rows // 2,), (rows // 4,), (rows // 4,)], lambda i: (0, i)
    if split == "x":
        blocks, index = [(N_Y, rows // (N_X * N_Y))] * N_X, lambda i: (0, 0, i)
    own, other = (pltpu.with_memory_space_constraint(w, pltpu.VMEM) for w in (own, other))
    return pl.pallas_call(
        functools.partial(project_kernel, start, split),
        grid=(STEPS,),
        in_specs=[WHOLE] * 3,
        out_specs=[pl.BlockSpec((*b, (end - start) // STEPS), index) for b in blocks],
        out_shape=[jax.ShapeDtypeStruct((*b, end - start), jnp.bfloat16) for b in blocks],
        compiler_params=pltpu.CompilerParams(vmem_limit_bytes=18 << 20),
        cost_estimate=pl.CostEstimate(
            flops=4 * rows * inner * (end - start),
            bytes_accessed=2 * rows * (end - start),
            transcendentals=0,
        ),
        name="project",
    )(values, own, other)


def split_sum_kernel(a_ref, b_ref, c_ref, *outs):
    rows = outs[0].shape[0]
    for dx, out in enumerate(outs):
        ref, at = (b_ref, dx) if dx < N_X // 2 else (c_ref, dx - N_X // 2)
        low = ref[at * rows : (at + 1) * rows].astype(jnp.float32)
        out[...] = (a_ref[dx * rows : (dx + 1) * rows].astype(jnp.float32) + low).astype(
            jnp.bfloat16
        )


def split_sum(a, b, c):
    part = jax.ShapeDtypeStruct((a.shape[0] // N_X, a.shape[1]), jnp.bfloat16)
    return pl.pallas_call(
        split_sum_kernel,
        in_specs=[WHOLE] * 3,
        out_specs=[WHOLE] * N_X,
        out_shape=[part] * N_X,
        compiler_params=pltpu.CompilerParams(vmem_limit_bytes=8 << 20),
        name="split_sum",
    )(a, b, c)


def pair_sum_kernel(a, b, c, d, keep, send):
    for dy, out in enumerate((keep, send)):
        total = a[dy].astype(jnp.float32) + b[dy].astype(jnp.float32)
        total = total + c[dy].astype(jnp.float32) + d[dy].astype(jnp.float32)
        out[...] = total.astype(jnp.bfloat16)


def pair_sum(parts):
    out = jax.ShapeDtypeStruct(parts[0].shape[1:], jnp.bfloat16)
    return pl.pallas_call(
        pair_sum_kernel,
        in_specs=[WHOLE] * len(parts),
        out_specs=[WHOLE] * 2,
        out_shape=[out] * 2,
        compiler_params=pltpu.CompilerParams(vmem_limit_bytes=8 << 20),
        name="pair_sum",
    )(*parts)


def finish_kernel(count, *refs):
    left, right, (residual, gain, hidden, normed) = refs[:2], refs[2:count], refs[count:]
    split = left[0].shape[1]
    squares = 0.0
    for parts, at in ((left, slice(0, split)), (right, slice(split, residual.shape[1]))):
        total = parts[0][...].astype(jnp.float32)
        for part in parts[1:]:
            total = total + part[...].astype(jnp.float32)
        low = (residual[:, at].astype(jnp.float32) + total).astype(jnp.bfloat16)
        hidden[:, at] = low
        wide = low.astype(jnp.float32)
        squares = squares + jnp.sum(wide * wide, axis=1, keepdims=True)
    factor = lax.rsqrt(squares / residual.shape[1] + epsilon)
    normed[...] = (
        hidden[...].astype(jnp.float32) * factor * gain[...].astype(jnp.float32)
    ).astype(jnp.bfloat16)


def finish(left, right, residual, gain):
    out = jax.ShapeDtypeStruct(residual.shape, jnp.bfloat16)
    count = len(left) + len(right)
    return pl.pallas_call(
        functools.partial(finish_kernel, count),
        in_specs=[WHOLE] * (count + 2),
        out_specs=[WHOLE] * 2,
        out_shape=[out] * 2,
        compiler_params=pltpu.CompilerParams(vmem_limit_bytes=8 << 20),
        name="finish",
    )(*left, *right, residual, gain.reshape(1, -1))


def per_device(queries, new_latent, latent_cache, lengths, residual, value_up, out_proj, norm_gain):
    latent = value_up.shape[1]
    width = out_proj.shape[1]
    flat_queries, flat_cache = (
        pltpu.with_memory_space_constraint(jnp.swapaxes(a, 1, 2), pltpu.HBM)
        for a in (queries, latent_cache)
    )
    new_latent = pltpu.with_memory_space_constraint(new_latent, pltpu.HBM)
    lengths = pltpu.with_memory_space_constraint(lengths, pltpu.HBM)
    other_proj = moved(out_proj, dcore=1)
    other_up = moved(value_up, dcore=1)
    blocks = list(attend(lengths, flat_queries, flat_cache, new_latent, latent))
    blocks[2], _ = lax.optimization_barrier((blocks[2], other_up))

    by_y = [blocks[N_X], moved(blocks[N_X + 1], dy=1)]
    by_x = [blocks[0]] + [moved(blocks[dx], dx=dx) for dx in range(1, N_X)]
    spread = regroup(by_y, [[(dy, dx) for dy in range(N_Y)] for dx in range(1, N_X)])
    spread = [moved(spread[dx - 1], dx=dx) for dx in range(1, N_X)]
    (crossed,) = regroup(by_x, [[(dx, 1) for dx in range(N_X)]])
    crossed = moved(crossed, dy=1)

    arrays = [*by_x, crossed, *by_y, *spread]
    own = [(dx, 0) for dx in range(N_X)] + [(N_X, dx) for dx in range(N_X)]
    other = []
    for dy in range(N_Y):
        other.append((N_X + 1 + dy, 0))
        other += [(N_X + 1 + N_Y + dx - 1, dy) for dx in range(1, N_X)]
    values = lift(arrays, (own, other), value_up, other_up)

    split = width * 4 // 7
    sums = project(values, out_proj, other_proj, 0, split, "x")
    left = [sums[0]] + [moved(sums[dx], dx=-dx) for dx in (1, 3, 2)]
    values, _ = lax.optimization_barrier((values, sums[0]))
    keep, *send = project(values, out_proj, other_proj, split, width, "y")
    right = split_sum(keep, *(moved(s, dy=1) for s in send))
    right = [right[0]] + [moved(right[dx], dx=-dx) for dx in (1, 3, 2)]
    mine, others = pair_sum(left)
    return tuple(finish([mine, moved(others, dy=1)], right, residual, norm_gain))


def solution(mesh):
    return jax.shard_map(
        per_device,
        mesh=mesh,
        in_specs=(
            P(("dp", "tp"), None, None),
            P(("dp", "tp"), None),
            P(("dp", "tp"), None, None),
            P(("dp", "tp")),
            P(("dp", "tp"), None),
            P("tp", None, None),
            P("tp", None),
            P(),
        ),
        out_specs=(P(("dp", "tp"), None), P(("dp", "tp"), None)),
        check_vma=False,
    )
```

```python
import functools

import jax
import jax.numpy as jnp
from jax import lax
from jax.experimental import pallas as pl
from jax.experimental.pallas import tpu as pltpu
from jax.sharding import PartitionSpec as P

softmax_scale = 0.1353
masked_score = -1e30
epsilon = 1e-06

N_X, N_Y, N_CORE = 4, 2, 2
STEP = 4
FLUSH = 16
STEPS = 2
WHOLE = pl.BlockSpec(memory_space=pltpu.VMEM)


def moved(array, dx=0, dy=0, dcore=0):
    pairs = []
    for t in range(N_X * N_Y * N_CORE):
        x, y, core = t // (N_Y * N_CORE), t // N_CORE % N_Y, t % N_CORE
        to = ((x + dx) % N_X * N_Y + (y ^ dy)) * N_CORE + (core ^ dcore)
        pairs.append((t, to))
    return lax.ppermute(array, "tp", pairs)


def attend_kernel(latent, len_ref, q_ref, c_ref, n_ref, *rest):
    outs, (stage, new_wide) = rest[:-2], rest[-2:]
    i = pl.program_id(0)
    heads, slots = q_ref.shape[2], c_ref.shape[2]
    rows = n_ref.shape[0]

    @pl.when(i == 0)
    def _():
        new_wide[...] = n_ref[...].astype(jnp.float32)

    def attend_to(seen):
        every = range(STEP)
        queries = [q_ref[j].T for j in every]
        keys = [c_ref[j, :, :seen] for j in every]
        news = [new_wide[pl.ds(i * STEP + j, 1), :] for j in every]
        scores = [
            jnp.dot(q, k, preferred_element_type=jnp.float32) * softmax_scale
            for q, k in zip(queries, keys)
        ]
        new_scores = [
            jnp.sum(q.astype(jnp.float32) * n, axis=1, keepdims=True) * softmax_scale
            for q, n in zip(queries, news)
        ]
        positions = lax.broadcasted_iota(jnp.int32, (1, seen), 1)
        masked = [
            jnp.where(positions < len_ref[i * STEP + j], scores[j], masked_score)
            for j in every
        ]
        maxima = [
            jnp.maximum(jnp.max(m, axis=1, keepdims=True), n) for m, n in zip(masked, new_scores)
        ]
        probs = [jnp.exp(m - top) for m, top in zip(masked, maxima)]
        new_probs = [jnp.exp(n - top) for n, top in zip(new_scores, maxima)]
        summed = [
            lax.dot_general(
                p.astype(jnp.bfloat16),
                k[:latent],
                (((1,), (1,)), ((), ())),
                preferred_element_type=jnp.float32,
            )
            for p, k in zip(probs, keys)
        ]
        inverse = [
            1.0 / (jnp.sum(p, axis=1, keepdims=True) + n) for p, n in zip(probs, new_probs)
        ]
        for j in every:
            new_low = new_probs[j].astype(jnp.bfloat16).astype(jnp.float32)
            attended = (summed[j] + new_low * news[j][:, :latent]) * inverse[j]
            for c in range(latent // 128):
                stage[c, pl.ds(i % (FLUSH // STEP) * STEP + j, heads, stride=FLUSH), :] = attended[
                    :, c * 128 : (c + 1) * 128
                ]

    longest = len_ref[i * STEP]
    for j in range(1, STEP):
        longest = jnp.maximum(longest, len_ref[i * STEP + j])
    for seen in range(128, slots + 1, 128):
        in_reach = (longest > seen - 128) & (longest <= seen)
        pl.when(in_reach)(functools.partial(attend_to, seen))

    def flush(begin):
        per = heads // (N_X * N_Y * N_CORE)
        t = lax.axis_index("tp")
        x, y, core = t // (N_Y * N_CORE), t // N_CORE % N_Y, t % N_CORE
        for dx in range(N_X):
            for dy in range(N_Y):
                chip = (x + dx) % N_X * N_Y + (y ^ dy)
                for out, to in ((outs[dx].at[dy], core), (outs[N_X + dy].at[dx], core ^ 1)):
                    at = pl.multiple_of((chip * N_CORE + to) * (per * FLUSH), per * FLUSH)
                    for c in range(latent // 128):
                        block = stage[c, pl.ds(at, per * FLUSH), :].reshape(per, FLUSH, 128)
                        out[:, begin : begin + FLUSH, c * 128 : (c + 1) * 128] = block.astype(
                            jnp.bfloat16
                        )

    for begin in range(0, rows, FLUSH):
        pl.when((i + 1) * STEP == begin + FLUSH)(functools.partial(flush, begin))


def attend(lengths, queries, cache, new, latent):
    rows, width, heads = queries.shape
    slots = cache.shape[2]
    block = (heads // (N_X * N_Y * N_CORE), rows, latent)
    shapes = [(N_Y, *block)] * N_X + [(N_X, *block)] * N_Y
    return pl.pallas_call(
        functools.partial(attend_kernel, latent),
        grid_spec=pltpu.PrefetchScalarGridSpec(
            num_scalar_prefetch=1,
            grid=(rows // STEP,),
            in_specs=[
                pl.BlockSpec((STEP, width, heads), lambda i, *_: (i, 0, 0)),
                pl.BlockSpec((STEP, width, slots), lambda i, *_: (i, 0, 0)),
                pl.BlockSpec((rows, width), lambda i, *_: (0, 0)),
            ],
            out_specs=[pl.BlockSpec(shape, lambda i, *_: (0, 0, 0, 0)) for shape in shapes],
            scratch_shapes=[
                pltpu.VMEM((latent // 128, heads * FLUSH, 128), jnp.float32),
                pltpu.VMEM((rows, width), jnp.float32),
            ],
        ),
        out_shape=[jax.ShapeDtypeStruct(shape, jnp.bfloat16) for shape in shapes],
        compiler_params=pltpu.CompilerParams(vmem_limit_bytes=18 << 20),
        cost_estimate=pl.CostEstimate(
            flops=8 * rows * heads * slots * (width + latent),
            bytes_accessed=2 * rows * (width * (slots + heads) + heads * latent),
            transcendentals=rows * heads * slots,
        ),
        name="attend",
    )(lengths, queries, cache, new)


def regroup_kernel(count, picks, *refs):
    ins, outs = refs[:count], refs[count:]
    for out, pick in zip(outs, picks):
        for to, (n, at) in enumerate(pick):
            out[to] = ins[n][at]


def regroup(arrays, picks):
    block = arrays[0].shape[1:]
    return pl.pallas_call(
        functools.partial(regroup_kernel, len(arrays), picks),
        in_specs=[WHOLE] * len(arrays),
        out_specs=[WHOLE] * len(picks),
        out_shape=[jax.ShapeDtypeStruct((len(p), *block), jnp.bfloat16) for p in picks],
        compiler_params=pltpu.CompilerParams(vmem_limit_bytes=8 << 20),
        name="regroup",
    )(*arrays)


def lift_kernel(count, picks, *refs):
    arrays, (own_up, other_up, values) = refs[:count], refs[count:]
    heads, _, depth = own_up.shape
    for s, up in enumerate((own_up, other_up)):
        for h in range(heads):
            rows = jnp.concatenate([arrays[n][at, h] for n, at in picks[s]], axis=0)
            lifted = jnp.dot(rows, up[h], preferred_element_type=jnp.float32)
            at = (s * heads + h) * depth
            values[:, at : at + depth] = lifted.astype(jnp.bfloat16)


def lift(arrays, picks, own_up, other_up):
    heads, latent, depth = own_up.shape
    rows = len(picks[0]) * arrays[0].shape[2]
    return pl.pallas_call(
        functools.partial(lift_kernel, len(arrays), picks),
        in_specs=[WHOLE] * (len(arrays) + 2),
        out_specs=WHOLE,
        out_shape=jax.ShapeDtypeStruct((rows, N_CORE * heads * depth), jnp.bfloat16),
        compiler_params=pltpu.CompilerParams(vmem_limit_bytes=10 << 20),
        cost_estimate=pl.CostEstimate(
            flops=4 * rows * heads * latent * depth,
            bytes_accessed=4 * rows * heads * latent,
            transcendentals=0,
        ),
        name="lift",
    )(*arrays, own_up, other_up)


def project_kernel(start, split, values, own_ref, other_ref, *outs):
    inner, width = own_ref.shape[0], outs[0].shape[-1]
    at = pl.ds(pl.multiple_of(start + pl.program_id(0) * width, 128), width)
    tile = jnp.dot(values[:, :inner], own_ref[:, at], preferred_element_type=jnp.float32)
    tile = tile + jnp.dot(values[:, inner:], other_ref[:, at], preferred_element_type=jnp.float32)
    tile = tile.astype(jnp.bfloat16)
    if split == "y":
        begin = 0
        for out in outs:
            out[...] = tile[begin : begin + out.shape[0]]
            begin += out.shape[0]
        return
    rows = tile.shape[0] // (N_X * N_Y)
    for dx, out in enumerate(outs):
        for dy in range(N_Y):
            begin = (dy * N_X + dx) * rows
            out[dy] = tile[begin : begin + rows]


def project(values, own, other, start, end, split):
    rows = values.shape[0]
    inner = own.shape[0]
    blocks, index = [(rows // 2,), (rows // 4,), (rows // 4,)], lambda i: (0, i)
    if split == "x":
        blocks, index = [(N_Y, rows // (N_X * N_Y))] * N_X, lambda i: (0, 0, i)
    own, other = (pltpu.with_memory_space_constraint(w, pltpu.VMEM) for w in (own, other))
    return pl.pallas_call(
        functools.partial(project_kernel, start, split),
        grid=(STEPS,),
        in_specs=[WHOLE] * 3,
        out_specs=[pl.BlockSpec((*b, (end - start) // STEPS), index) for b in blocks],
        out_shape=[jax.ShapeDtypeStruct((*b, end - start), jnp.bfloat16) for b in blocks],
        compiler_params=pltpu.CompilerParams(vmem_limit_bytes=18 << 20),
        cost_estimate=pl.CostEstimate(
            flops=4 * rows * inner * (end - start),
            bytes_accessed=2 * rows * (end - start),
            transcendentals=0,
        ),
        name="project",
    )(values, own, other)


def split_sum_kernel(a_ref, b_ref, c_ref, *outs):
    rows = outs[0].shape[0]
    for dx, out in enumerate(outs):
        ref, at = (b_ref, dx) if dx < N_X // 2 else (c_ref, dx - N_X // 2)
        low = ref[at * rows : (at + 1) * rows].astype(jnp.float32)
        out[...] = (a_ref[dx * rows : (dx + 1) * rows].astype(jnp.float32) + low).astype(
            jnp.bfloat16
        )


def split_sum(a, b, c):
    part = jax.ShapeDtypeStruct((a.shape[0] // N_X, a.shape[1]), jnp.bfloat16)
    return pl.pallas_call(
        split_sum_kernel,
        in_specs=[WHOLE] * 3,
        out_specs=[WHOLE] * N_X,
        out_shape=[part] * N_X,
        compiler_params=pltpu.CompilerParams(vmem_limit_bytes=8 << 20),
        name="split_sum",
    )(a, b, c)


def pair_sum_kernel(a, b, c, d, keep, *send):
    for dy in range(N_Y):
        total = a[dy].astype(jnp.float32) + b[dy].astype(jnp.float32)
        total = total + c[dy].astype(jnp.float32) + d[dy].astype(jnp.float32)
        total = total.astype(jnp.bfloat16)
        if dy == 0:
            keep[...] = total
            continue
        width = send[0].shape[1]
        for n, out in enumerate(send):
            out[...] = total[:, n * width : (n + 1) * width]


def pair_sum(parts):
    _, rows, width = parts[0].shape
    outs = [jax.ShapeDtypeStruct((rows, w), jnp.bfloat16) for w in (width, width // 2, width // 2)]
    return pl.pallas_call(
        pair_sum_kernel,
        in_specs=[WHOLE] * len(parts),
        out_specs=[WHOLE] * 3,
        out_shape=outs,
        compiler_params=pltpu.CompilerParams(vmem_limit_bytes=8 << 20),
        name="pair_sum",
    )(*parts)


def finish_kernel(count, *refs):
    (mine, *pieces), right, (residual, gain, hidden, normed) = refs[:3], refs[3:count], refs[count:]
    split, width = mine.shape[1], pieces[0].shape[1]
    columns = [slice(n * width, (n + 1) * width) for n in range(len(pieces))]
    sums = [([mine.at[:, at], piece], at) for piece, at in zip(pieces, columns)]
    sums.append((right, slice(split, residual.shape[1])))
    squares = 0.0
    for parts, at in sums:
        total = parts[0][...].astype(jnp.float32)
        for part in parts[1:]:
            total = total + part[...].astype(jnp.float32)
        low = (residual[:, at].astype(jnp.float32) + total).astype(jnp.bfloat16)
        hidden[:, at] = low
        wide = low.astype(jnp.float32)
        squares = squares + jnp.sum(wide * wide, axis=1, keepdims=True)
    factor = lax.rsqrt(squares / residual.shape[1] + epsilon)
    normed[...] = (
        hidden[...].astype(jnp.float32) * factor * gain[...].astype(jnp.float32)
    ).astype(jnp.bfloat16)


def finish(left, right, residual, gain):
    out = jax.ShapeDtypeStruct(residual.shape, jnp.bfloat16)
    count = len(left) + len(right)
    return pl.pallas_call(
        functools.partial(finish_kernel, count),
        in_specs=[WHOLE] * (count + 2),
        out_specs=[WHOLE] * 2,
        out_shape=[out] * 2,
        compiler_params=pltpu.CompilerParams(vmem_limit_bytes=8 << 20),
        name="finish",
    )(*left, *right, residual, gain.reshape(1, -1))


def per_device(queries, new_latent, latent_cache, lengths, residual, value_up, out_proj, norm_gain):
    latent = value_up.shape[1]
    width = out_proj.shape[1]
    flat_queries, flat_cache = (
        pltpu.with_memory_space_constraint(jnp.swapaxes(a, 1, 2), pltpu.HBM)
        for a in (queries, latent_cache)
    )
    new_latent = pltpu.with_memory_space_constraint(new_latent, pltpu.HBM)
    lengths = pltpu.with_memory_space_constraint(lengths, pltpu.HBM)
    other_proj = moved(out_proj, dcore=1)
    other_up = moved(value_up, dcore=1)
    blocks = list(attend(lengths, flat_queries, flat_cache, new_latent, latent))
    blocks[2], _ = lax.optimization_barrier((blocks[2], other_up))

    by_y = [blocks[N_X], moved(blocks[N_X + 1], dy=1)]
    by_x = [blocks[0]] + [moved(blocks[dx], dx=dx) for dx in range(1, N_X)]
    spread = regroup(by_y, [[(dy, dx) for dy in range(N_Y)] for dx in range(1, N_X)])
    spread = [moved(spread[dx - 1], dx=dx) for dx in range(1, N_X)]
    (crossed,) = regroup(by_x, [[(dx, 1) for dx in range(N_X)]])
    crossed = moved(crossed, dy=1)

    arrays = [*by_x, crossed, *by_y, *spread]
    own = [(dx, 0) for dx in range(N_X)] + [(N_X, dx) for dx in range(N_X)]
    other = []
    for dy in range(N_Y):
        other.append((N_X + 1 + dy, 0))
        other += [(N_X + 1 + N_Y + dx - 1, dy) for dx in range(1, N_X)]
    values = lift(arrays, (own, other), value_up, other_up)

    split = width * 17 // 28
    sums = project(values, out_proj, other_proj, 0, split, "x")
    left = [sums[0]] + [moved(sums[dx], dx=-dx) for dx in (1, 3, 2)]
    values, _ = lax.optimization_barrier((values, sums[0]))
    keep, *send = project(values, out_proj, other_proj, split, width, "y")
    right = split_sum(keep, *(moved(s, dy=1) for s in send))
    right = [right[0]] + [moved(right[dx], dx=-dx) for dx in (1, 3, 2)]
    mine, *others = pair_sum(left)
    left = [mine] + [moved(o, dy=1) for o in others]
    return tuple(finish(left, right, residual, norm_gain))


def solution(mesh):
    return jax.shard_map(
        per_device,
        mesh=mesh,
        in_specs=(
            P(("dp", "tp"), None, None),
            P(("dp", "tp"), None),
            P(("dp", "tp"), None, None),
            P(("dp", "tp")),
            P(("dp", "tp"), None),
            P("tp", None, None),
            P("tp", None),
            P(),
        ),
        out_specs=(P(("dp", "tp"), None), P(("dp", "tp"), None)),
        check_vma=False,
    )
```
